32 devices in a mesh: dp: 16 (over z, y, core), fsdp: 2 (over x).
Axes of the slice: x: 2, y: 2, z: 4, core: 2. Of those that a mesh axis runs over, the one named last changes fastest.
Arguments:
- tokens: bfloat16 [4096, 576], P(('dp', 'fsdp')), may hold values from -6 to 6
- segments: int32 [4096], P(('dp', 'fsdp')), may hold values from -1 to 4095, as said below
- cotangent: bfloat16 [4096, 576], P(('dp', 'fsdp')), may hold values from -6 to 6
- attn_gain: bfloat16 [2, 576], P(None, 'dp'), may hold values from 0.5 to 1.5
- w_query: bfloat16 [2, 576, 576], P(None, 'dp', 'fsdp'), may hold values from -0.375 to 0.375
- w_key: bfloat16 [2, 576, 192], P(None, 'dp', 'fsdp'), may hold values from -0.25 to 0.25
- w_value: bfloat16 [2, 576, 192], P(None, 'dp', 'fsdp'), may hold values from -0.25 to 0.25
- w_out: bfloat16 [2, 576, 576], P(None, 'dp', 'fsdp'), may hold values from -1 to 1
- mlp_gain: bfloat16 [2, 576], P(None, 'dp'), may hold values from 0.5 to 1.5
- w_gate: bfloat16 [2, 576, 1536], P(None, 'dp', 'fsdp'), may hold values from -0.25 to 0.25
- w_up: bfloat16 [2, 576, 1536], P(None, 'dp', 'fsdp'), may hold values from -0.25 to 0.25
- w_down: bfloat16 [2, 1536, 576], P(None, 'dp', 'fsdp'), may hold values from -0.15625 to 0.15625
Outputs:
- output: bfloat16 [4096, 576], P(('dp', 'fsdp'))
- grad_tokens: float32 [4096, 576], P(('dp', 'fsdp'))
- grad_attn_gain: float32 [2, 576], P(None, 'dp')
- grad_w_query: float32 [2, 576, 576], P(None, 'dp', 'fsdp')
- grad_w_key: float32 [2, 576, 192], P(None, 'dp', 'fsdp')
- grad_w_value: float32 [2, 576, 192], P(None, 'dp', 'fsdp')
- grad_w_out: float32 [2, 576, 576], P(None, 'dp', 'fsdp')
- grad_mlp_gain: float32 [2, 576], P(None, 'dp')
- grad_w_gate: float32 [2, 576, 1536], P(None, 'dp', 'fsdp')
- grad_w_up: float32 [2, 576, 1536], P(None, 'dp', 'fsdp')
- grad_w_down: float32 [2, 1536, 576], P(None, 'dp', 'fsdp')
The draws below stay inside these ranges and needn't reach their ends.
Inputs may be any that keep to these rules, and one draw needn't show every extreme that they name: `segments`: each block of 128 rows of one device holds whole sequences in a prefix of its rows and -1 in the rest, with 64 live rows or more; a sequence's rows are consecutive and carry the index of its first row in the whole array; in every draw one block holds a single sequence of 128 rows, the longest.
All inputs are finite; a program needn't handle non-finite values.
Results may differ from the reference program's by a relative error of at most 0.025.
Values may be sent and summed in bfloat16 or wider, within the bound.
A program may use at most 128 MiB of HBM per device.

```python
import math
import jax
import jax.numpy as jnp
from jax import lax

D = 576
FF = 1536
HEADS_Q = 9
HEADS_KV = 3
HEAD = 64
LAYERS = 2
TOK_DEV = 128
TOKENS = 4096


def draw_segments(key, part):
    key = jax.random.fold_in(key, 11)
    blocks = TOKENS // TOK_DEV
    key_live, key_full, key_cuts = jax.random.split(key, 3)
    live = jax.random.randint(key_live, (blocks,), TOK_DEV // 2, TOK_DEV + 1)
    full = jax.random.randint(key_full, (), 0, blocks)
    rows = jnp.arange(TOK_DEV, dtype=jnp.int32)
    starts = jax.random.randint(key_cuts, (blocks, TOK_DEV), 0, TOK_DEV) < 3
    starts = starts | (rows[None, :] == 0)
    is_full = jnp.arange(blocks, dtype=jnp.int32) == full
    live = jnp.where(is_full, TOK_DEV, live)
    starts = jnp.where(is_full[:, None], rows[None, :] == 0, starts)
    first = lax.cummax(jnp.where(starts, rows[None, :], 0), axis=1)
    ident = first + (jnp.arange(blocks, dtype=jnp.int32) * TOK_DEV)[:, None]
    ident = jnp.where(rows[None, :] < live[:, None], ident, -1)
    return ident.reshape(TOKENS).astype(jnp.int32)


def steps_of(rng, shape, shards, least, largest):
    level = 1.0
    for axis_at, blocks in shards:
        steps = jax.random.uniform(jax.random.fold_in(jax.random.fold_in(rng, 6), axis_at), (blocks,), jnp.float32, least / len(shards), largest / len(shards))
        level = level * jnp.repeat(jnp.exp(steps), shape[axis_at] // blocks).reshape((-1,) + (1,) * (len(shape) - 1 - axis_at))
    return level


def scatter_about(own_key, extent, deviation, most, cuts=(), kind=jnp.bfloat16):
    values = deviation * jax.random.normal(own_key, extent, jnp.float32)
    if cuts:
        values = values * steps_of(own_key, extent, cuts, -0.22, 0.18)
    return jnp.clip(values, -most, most).astype(kind)


def setup_inputs(seed: int = 0) -> dict:
    key_list = jax.random.split(jax.random.key(seed), 13)
    tokens = scatter_about(key_list[0], (TOKENS, D), 1.0, 6.0, ((0, 32),))
    segments = draw_segments(jax.random.fold_in(key_list[12], 71), 0)
    cotangent = scatter_about(key_list[2], (TOKENS, D), 1.0, 6.0, ((0, 32),))
    attn_gain = jnp.clip(1.0 + 0.1 * jax.random.normal(key_list[3], (LAYERS, D), jnp.float32), 0.5, 1.5).astype(jnp.bfloat16)
    w_query = scatter_about(key_list[4], (LAYERS, D, HEADS_Q * HEAD), (D // 2) ** -0.5, 0.375, ((1, 16), (2, 2)))
    w_key = scatter_about(key_list[5], (LAYERS, D, HEADS_KV * HEAD), D ** -0.5, 0.25, ((1, 16), (2, 2)))
    w_value = scatter_about(key_list[6], (LAYERS, D, HEADS_KV * HEAD), D ** -0.5, 0.25, ((1, 16), (2, 2)))
    w_out = scatter_about(key_list[7], (LAYERS, HEADS_Q * HEAD, D), (HEADS_Q * HEAD // 16) ** -0.5, 1.0, ((1, 16), (2, 2)))
    mlp_gain = jnp.clip(1.0 + 0.1 * jax.random.normal(key_list[8], (LAYERS, D), jnp.float32), 0.5, 1.5).astype(jnp.bfloat16)
    w_gate = scatter_about(key_list[9], (LAYERS, D, FF), D ** -0.5, 0.25, ((1, 16), (2, 2)))
    w_up = scatter_about(key_list[10], (LAYERS, D, FF), D ** -0.5, 0.25, ((1, 16), (2, 2)))
    w_down = scatter_about(key_list[11], (LAYERS, FF, D), FF ** -0.5, 0.15625, ((1, 16), (2, 2)))
    return dict(tokens=tokens, segments=segments, cotangent=cotangent, attn_gain=attn_gain, w_query=w_query, w_key=w_key, w_value=w_value, w_out=w_out, mlp_gain=mlp_gain, w_gate=w_gate, w_up=w_up, w_down=w_down)


EPS = 1e-05
ROPE_BASE = 100000.0
NEGATIVE = -1e+30
HIGH = lax.Precision.HIGHEST

@jax.custom_vjp
def low(v):
    return lax.optimization_barrier(v.astype(jnp.bfloat16)).astype(jnp.float32)

@jax.custom_vjp
def low_back(v):
    return v

def low_keep(v):
    return (low(v), None)

def low_pass(kept, grad):
    return (grad,)

def back_keep(v):
    return (v, None)

def back_low(kept, grad):
    return (low(grad),)
low.defvjp(low_keep, low_pass)
low_back.defvjp(back_keep, back_low)

def matmul(left, right):
    return jnp.dot(left, right, precision=HIGH, preferred_element_type=jnp.float32)

def rms_scale(source, gain):
    return source * lax.rsqrt(lax.optimization_barrier(jnp.mean(source * source, axis=-1, keepdims=True)) + EPS) * gain

def block_tables(segment_block):
    rows = segment_block.shape[0]
    index = jnp.arange(rows, dtype=jnp.int32)
    same = segment_block[:, None] == segment_block[None, :]
    allowed = same & (index[None, :] <= index[:, None])
    position = lax.optimization_barrier(jnp.sum((same & (index[None, :] < index[:, None])).astype(jnp.int32), axis=1))
    half = HEAD // 2
    freq = ROPE_BASE ** (-(2.0 * jnp.arange(half, dtype=jnp.float32)) / HEAD)
    angle = position.astype(jnp.float32)[:, None] * freq[None, :]
    return (allowed, jnp.cos(angle), jnp.sin(angle))

def rotate(heads, cosine, sine):
    half = HEAD // 2
    first = heads[..., :half]
    second = heads[..., half:]
    c = cosine[:, None, :]
    s = sine[:, None, :]
    return jnp.concatenate([first * c - second * s, second * c + first * s], axis=-1)

def attend_block(inputs):
    query, keys, values, segment_block = inputs
    rows = query.shape[0]
    group = HEADS_Q // HEADS_KV
    scale = 1.0 / math.sqrt(HEAD)
    allowed, cosine, sine = block_tables(segment_block)
    query_rot = low(rotate(query.reshape(rows, HEADS_Q, HEAD), cosine, sine))
    key_rot = low(rotate(keys.reshape(rows, HEADS_KV, HEAD), cosine, sine))
    grouped = query_rot.reshape(rows, HEADS_KV, group, HEAD)
    scores = low_back(jnp.einsum('qhgd,khd->hgqk', grouped, key_rot, precision=HIGH) * scale)
    scores = jnp.where(allowed[None, None], scores, NEGATIVE)
    top = lax.optimization_barrier(jnp.max(scores, axis=-1, keepdims=True))
    unnormed = jnp.exp(scores - top)
    probs = low(unnormed / lax.optimization_barrier(jnp.sum(unnormed, axis=-1, keepdims=True)))
    mixed = jnp.einsum('hgqk,khd->qhgd', probs, values.reshape(rows, HEADS_KV, HEAD), precision=HIGH)
    return mixed.reshape(rows, HEADS_Q * HEAD)

def to_blocks(array, blocks):
    return array.reshape(blocks, TOK_DEV, array.shape[-1])

def layer(state, segment_blocks, weights):
    gain_attn, w_query, w_key, w_value, w_out, gain_mlp, w_gate, w_up, w_down = weights
    rows = state.shape[0]
    blocks = segment_blocks.shape[0]
    normed = low(rms_scale(state, gain_attn))
    query = low_back(matmul(normed, w_query))
    keys = low_back(matmul(normed, w_key))
    values = low(low_back(matmul(normed, w_value)))
    mixed = lax.map(jax.checkpoint(attend_block), (to_blocks(query, blocks), to_blocks(keys, blocks), to_blocks(values, blocks), segment_blocks))
    mixed = low_back(low(mixed.reshape(rows, HEADS_Q * HEAD)))
    resid = state + low_back(matmul(mixed, w_out))
    normed2 = low(rms_scale(resid, gain_mlp))
    gate = low_back(matmul(normed2, w_gate))
    lifted = low_back(matmul(normed2, w_up))
    hidden = low(gate * jax.nn.sigmoid(gate) * lifted)
    return resid + low_back(matmul(hidden, w_down))

def forward(state, segment_blocks, params):
    for level in range(LAYERS):
        state = layer(state, segment_blocks, tuple((item[level] for item in params)))
    return state

def reference(tokens, segments, cotangent, attn_gain, w_query, w_key, w_value, w_out, mlp_gain, w_gate, w_up, w_down):
    blocks_all = TOKENS // TOK_DEV
    per_group = math.gcd(blocks_all, max(1, 4096 // TOK_DEV))
    groups = blocks_all // per_group
    span = per_group * TOK_DEV
    params = tuple((item.astype(jnp.float32) for item in (attn_gain, w_query, w_key, w_value, w_out, mlp_gain, w_gate, w_up, w_down)))

    def group_step(totals, inputs):
        rows_in, segment_rows, cot_rows = inputs
        segment_blocks = segment_rows.reshape(per_group, TOK_DEV)
        live = (segment_rows >= 0).astype(jnp.float32)[:, None]
        state = rows_in.astype(jnp.float32)

        def run(start, weights):
            return forward(start, segment_blocks, weights)
        result, pullback = jax.vjp(run, state, params)
        grad_state, grad_params = pullback(cot_rows.astype(jnp.float32) * live)
        totals = jax.tree.map(lambda a, b: a + b, totals, grad_params)
        return (totals, (result.astype(jnp.bfloat16), grad_state))
    zeros = jax.tree.map(jnp.zeros_like, params)
    totals, stacked = lax.scan(group_step, zeros, (tokens.reshape(groups, span, D), segments.reshape(groups, span), cotangent.reshape(groups, span, D)))
    output = stacked[0].reshape(TOKENS, D)
    grad_tokens = stacked[1].reshape(TOKENS, D)
    return (output, grad_tokens, totals[0], totals[1], totals[2], totals[3], totals[4], totals[5], totals[6], totals[7], totals[8])
```

```python
import functools
import math

import jax
import jax.numpy as jnp
from jax import lax
from jax.experimental import pallas as pl
from jax.experimental.pallas import tpu as pltpu
from jax.sharding import PartitionSpec as P

HEADS_Q = 9
HEADS_KV = 3
HEAD = 64
LAYERS = 2


EPS = 1e-05
ROPE_BASE = 100000.0
NEGATIVE = -1e30


def product(left, right):
    return jnp.dot(left, right, preferred_element_type=jnp.float32)


def outer_rows(left, right):
    return lax.dot_general(
        left, right, (((0,), (0,)), ((), ())), preferred_element_type=jnp.float32
    )


def back_product(left, right):
    return lax.dot_general(
        left, right, (((1,), (1,)), ((), ())), preferred_element_type=jnp.float32
    )


def rms_scale(source, gain):
    return source * lax.rsqrt(jnp.mean(source * source, axis=-1, keepdims=True) + EPS) * gain


def norm_back(grad_normed, source, gain):
    root = lax.rsqrt(jnp.mean(source * source, axis=-1, keepdims=True) + EPS)
    unit = source * root
    scaled = grad_normed * gain
    grad_gain = jnp.sum(grad_normed * unit, axis=0)
    grad_source = root * (scaled - unit * jnp.mean(scaled * unit, axis=-1, keepdims=True))
    return (grad_source, grad_gain)


def tables(segments):
    rows = segments.shape[0]
    index = jnp.arange(rows, dtype=jnp.int32)
    same = segments[:, None] == segments[None, :]
    allowed = same & (index[None, :] <= index[:, None])
    position = jnp.sum((same & (index[None, :] < index[:, None])).astype(jnp.int32), axis=1)
    half = HEAD // 2
    freq = ROPE_BASE ** (-(2.0 * jnp.arange(half, dtype=jnp.float32)) / HEAD)
    angle = position.astype(jnp.float32)[:, None] * freq[None, :]
    return (allowed, jnp.cos(angle), jnp.sin(angle))


def rotate(heads, cosine, sine):
    half = HEAD // 2
    first = heads[..., :half]
    second = heads[..., half:]
    c = cosine[:, None, :]
    s = sine[:, None, :]
    return jnp.concatenate([first * c - second * s, second * c + first * s], axis=-1)


def rotate_back(grads, cosine, sine):
    half = HEAD // 2
    first = grads[..., :half]
    second = grads[..., half:]
    c = cosine[:, None, :]
    s = sine[:, None, :]
    return jnp.concatenate([first * c + second * s, second * c - first * s], axis=-1)


MESH = pl.DeviceIdType.MESH
VMEM_BYTES = 56 * 1024 * 1024


def bit_count(size):
    return size.bit_length() - 1


def exchange_orders():
    high = [("dp", bit) for bit in range(bit_count(lax.axis_size("dp")) - 1, -1, -1)]
    far, near, core = high[:-2], high[-2:-1], high[-1:]
    across = [("fsdp", bit) for bit in range(bit_count(lax.axis_size("fsdp")) - 1, -1, -1)]
    return (far + near + across + core, far + across + near + core)


def bit_of(index, bit):
    return lax.rem(lax.div(index, 1 << bit), 2)


def partner_of(spot):
    axis, bit = spot
    index = lax.axis_index(axis)
    return {axis: index + (1 - 2 * bit_of(index, bit)) * (1 << bit)}


def greet(order):
    barrier = pltpu.get_barrier_semaphore()
    for spot in order:
        pl.semaphore_signal(barrier, inc=1, device_id=partner_of(spot), device_id_type=MESH)
    pl.semaphore_wait(barrier, len(order))


def gather_kernel(orders, *refs):
    first, second, gains, all_first, all_second, all_gains, own_sem, send_sem, recv_sem = refs
    steps = len(orders[0])
    pieces = []
    for source, target, order in ((first, all_first, orders[0]), (second, all_second, orders[1])):
        for half in range(2):
            pieces.append(
                (source.at[half], lambda at, n, t=target, h=half: t.at[pl.ds(at, n), h], order)
            )
    whole = gains.shape[0]
    pieces.insert(
        0,
        (
            gains.at[pl.ds(0, whole)],
            lambda at, n: all_gains.at[pl.ds(at * whole, n * whole)],
            orders[0],
        ),
    )
    greet(orders[0])
    slots = []
    for order in orders:
        slot = 0
        for step, (axis, bit) in enumerate(order):
            slot = slot + bit_of(lax.axis_index(axis), bit) * (1 << step)
        slots.append(slot)
    slot_for = [slots[0], slots[0], slots[0], slots[1], slots[1]]
    own = []
    for k, (source, view, order) in enumerate(pieces):
        copy = pltpu.make_async_copy(source, view(slot_for[k], 1) if k == 0 else
                                     view(slot_for[k], 1).at[0], own_sem.at[k])
        copy.start()
        own.append(copy)
    sent = []
    previous = [None] * len(pieces)
    for step in range(steps):
        for k, (source, view, order) in enumerate(pieces):
            if step == 0:
                own[k].wait()
            else:
                previous[k].wait_recv()
            base = lax.div(slot_for[k], 1 << step) * (1 << step)
            block = view(base, 1 << step)
            copy = pltpu.make_async_remote_copy(
                src_ref=block,
                dst_ref=block,
                send_sem=send_sem.at[k, step],
                recv_sem=recv_sem.at[k, step],
                device_id=partner_of(order[step]),
                device_id_type=MESH,
            )
            copy.start()
            sent.append(copy)
            previous[k] = copy
    for copy in previous:
        copy.wait_recv()
    for copy in sent:
        copy.wait_send()


def gather_all(first, second, gains):
    orders = exchange_orders()
    count = lax.axis_size("dp") * lax.axis_size("fsdp")
    steps = len(orders[0])
    return pl.pallas_call(
        functools.partial(gather_kernel, orders),
        out_shape=(
            jax.ShapeDtypeStruct((count,) + first.shape, first.dtype),
            jax.ShapeDtypeStruct((count,) + second.shape, second.dtype),
            jax.ShapeDtypeStruct((count * gains.shape[0],) + gains.shape[1:], gains.dtype),
        ),
        in_specs=[pl.BlockSpec(memory_space=pl.ANY)] * 3,
        out_specs=[pl.BlockSpec(memory_space=pl.ANY)] * 3,
        scratch_shapes=[
            pltpu.SemaphoreType.DMA((5,)),
            pltpu.SemaphoreType.DMA((5, steps)),
            pltpu.SemaphoreType.DMA((5, steps)),
        ],
        compiler_params=pltpu.CompilerParams(collective_id=0, has_side_effects=True),
        name="gather_all",
    )(first, second, gains)


def scatter_kernel(orders, *refs):
    sources = refs[0:3]
    results = refs[3:6]
    totals = refs[6:11]
    arrived = refs[11:16]
    own_sem, send_sem, recv_sem = refs[16:19]
    steps = len(orders[0])
    pieces = [(0, 0, orders[0]), (0, 1, orders[0]), (1, 0, orders[1]), (1, 1, orders[1])]
    pieces.append((2, None, orders[0]))
    greet(orders[0])

    def send(k, step, block):
        n = 1 << step
        copy = pltpu.make_async_remote_copy(
            src_ref=block,
            dst_ref=arrived[k].at[pl.ds(n, n)],
            send_sem=send_sem.at[k, step],
            recv_sem=recv_sem.at[k, step],
            device_id=partner_of(pieces[k][2][step]),
            device_id_type=MESH,
        )
        copy.start()
        return copy

    def add(k, at, from_at, n):
        total, landed = totals[k], arrived[k]

        def body(i, carry):
            value = total[at + i].astype(jnp.float32) + landed[from_at + i].astype(jnp.float32)
            total[at + i] = value.astype(total.dtype)
            return carry

        lax.fori_loop(0, n, body, 0)

    top = steps - 1
    own, last, sent, places = [], [], [], []
    for k, (which, half, order) in enumerate(pieces):
        source = sources[which]
        axis, bit = order[top]
        mine = bit_of(lax.axis_index(axis), bit)
        n = 1 << top

        def view(at, source=source, half=half, n=n):
            return source.at[pl.ds(at, n)] if half is None else source.at[pl.ds(at, n), half]

        copy = send(k, top, view((1 - mine) * n))
        last.append(copy)
        sent.append(copy)
        keep = pltpu.make_async_copy(view(mine * n), totals[k], own_sem.at[k])
        keep.start()
        own.append(keep)
        places.append(0)
    for step in range(top, -1, -1):
        for k, (which, half, order) in enumerate(pieces):
            if step == top:
                own[k].wait()
            last[k].wait_recv()
            n = 1 << step
            at = places[k]
            if step > 0:
                axis, bit = order[step - 1]
                mine = bit_of(lax.axis_index(axis), bit)
                part = n // 2
                go, stay = (1 - mine) * part, mine * part
                add(k, at + go, n + go, part)
                last[k] = send(k, step - 1, totals[k].at[pl.ds(at + go, part)])
                sent.append(last[k])
                add(k, at + stay, n + stay, part)
                places[k] = at + stay
            else:
                value = totals[k][at].astype(jnp.float32) + arrived[k][1].astype(jnp.float32)
                if half is None:
                    results[which][...] = value
                else:
                    results[which][half] = value
    for copy in sent:
        copy.wait_send()


def scatter_all(first, second, gains):
    orders = exchange_orders()
    count = first.shape[0]
    steps = len(orders[0])
    piece = first.shape[2:]
    small = gains.shape[1:]
    halves = [pltpu.VMEM((count // 2,) + piece, first.dtype)] * 4
    fulls = [pltpu.VMEM((count,) + piece, first.dtype)] * 4
    return pl.pallas_call(
        functools.partial(scatter_kernel, orders),
        out_shape=(
            jax.ShapeDtypeStruct(first.shape[1:], jnp.float32),
            jax.ShapeDtypeStruct(second.shape[1:], jnp.float32),
            jax.ShapeDtypeStruct(small, jnp.float32),
        ),
        in_specs=[pl.BlockSpec(memory_space=pl.ANY)] * 3,
        out_specs=[pl.BlockSpec(memory_space=pltpu.VMEM)] * 3,
        scratch_shapes=halves
        + [pltpu.VMEM((count // 2,) + small, gains.dtype)]
        + fulls
        + [pltpu.VMEM((count,) + small, gains.dtype)]
        + [
            pltpu.SemaphoreType.DMA((5,)),
            pltpu.SemaphoreType.DMA((5, steps)),
            pltpu.SemaphoreType.DMA((5, steps)),
        ],
        compiler_params=pltpu.CompilerParams(
            collective_id=1, has_side_effects=True, vmem_limit_bytes=VMEM_BYTES
        ),
        name="scatter_all",
    )(first, second, gains)


def bit_axes(order):
    steps = len(order)
    spots = {spot: steps - 1 - step for step, spot in enumerate(order)}
    dp = [spots[spot] for spot in sorted(s for s in spots if s[0] == "dp")][::-1]
    fsdp = [spots[spot] for spot in sorted(s for s in spots if s[0] == "fsdp")][::-1]
    return (dp, fsdp)


def from_slots(slots, order, rows, columns):
    dp, fsdp = bit_axes(order)
    steps = len(order)
    split = slots.reshape((2,) * steps + slots.shape[1:])
    return split.transpose(
        dp + [steps + axis for axis in rows] + fsdp + [steps + axis for axis in columns]
    )


def to_slots(whole, order, rest, rows, columns):
    dp, fsdp = bit_axes(order)
    steps = len(order)
    forward = dp + [steps + axis for axis in rows] + fsdp + [steps + axis for axis in columns]
    shape = [2 if axis < steps else rest[axis - steps] for axis in forward]
    inverse = [forward.index(axis) for axis in range(len(forward))]
    return whole.reshape(shape).transpose(inverse).reshape((1 << steps,) + tuple(rest))


def padded_rows(rows):
    return -(-rows // 16) * 16


def pack(w_query, w_key, w_value, w_out, w_gate, w_up, w_down):
    rows, columns = w_gate.shape
    attn = jnp.concatenate([w_query, w_key, w_value, w_out], axis=1)
    down = w_down.reshape(8, rows // 3, 3, columns // 8).transpose(2, 1, 0, 3)
    down = down.reshape(rows, columns)
    packed = jnp.concatenate([attn, w_gate, w_up, down], axis=0)
    packed = jnp.pad(packed, ((0, padded_rows(4 * rows) - 4 * rows), (0, 0)))
    return packed.reshape(-1, 2, columns // 2).transpose(1, 0, 2)


def unpack_shard(packed, rows, widths):
    half = packed.shape[2]
    columns = 2 * half
    wide = [
        jnp.concatenate([packed[0, m * rows : (m + 1) * rows], packed[1, m * rows : (m + 1) * rows]], axis=1)
        for m in range(4)
    ]
    q, k, v, o = widths
    attn = wide[0]
    down = wide[3].reshape(3, rows // 3, 8, columns // 8).transpose(2, 1, 0, 3)
    return (
        attn[:, :q],
        attn[:, q : q + k],
        attn[:, q + k : q + k + v],
        attn[:, q + k + v :],
        wide[1],
        wide[2],
        down.reshape(rows * 8 // 3, columns * 3 // 8),
    )


def unpack_all(slots, order, rows, widths):
    half = slots.shape[3]
    q, k, v, o = widths
    width = slots.shape[0] * rows // (1 << len(bit_axes(order)[1]))
    parts = [slots[:, :, m * rows : (m + 1) * rows] for m in range(4)]

    def attn(side, low, high):
        return from_slots(parts[0][:, side, :, low:high], order, [0], [1]).reshape(width, -1)

    gate = from_slots(parts[1], order, [1], [0, 2]).reshape(width, -1)
    up = from_slots(parts[2], order, [1], [0, 2]).reshape(width, -1)
    down = parts[3].reshape(-1, 2, 3, rows // 3, 4, half // 4)
    down = from_slots(down, order, [0, 3, 2], [1, 4]).reshape(-1, width)
    return (
        attn(0, 0, q),
        attn(0, q, q + k),
        attn(1, 0, v),
        attn(1, v, v + o),
        gate,
        up,
        down,
    )


def pack_all(grads, order, rows, widths, half):
    g_query, g_key, g_value, g_out, g_gate, g_up, g_down = [
        item.astype(jnp.bfloat16) for item in grads
    ]
    q, k, v, o = widths
    left = jnp.concatenate(
        [to_slots(g_query, order, [rows, q], [0], [1]), to_slots(g_key, order, [rows, k], [0], [1])],
        axis=2,
    )
    right = jnp.concatenate(
        [to_slots(g_value, order, [rows, v], [0], [1]), to_slots(g_out, order, [rows, o], [0], [1])],
        axis=2,
    )
    attn = jnp.stack([left, right], axis=1)
    gate = to_slots(g_gate, order, [2, rows, half], [1], [0, 2])
    up = to_slots(g_up, order, [2, rows, half], [1], [0, 2])
    down = to_slots(g_down, order, [2, 3, rows // 3, 4, half // 4], [0, 3, 2], [1, 4])
    down = down.reshape(-1, 2, rows, half)
    packed = jnp.concatenate([attn, gate, up, down], axis=2)
    return jnp.pad(packed, ((0, 0), (0, 0), (0, padded_rows(4 * rows) - 4 * rows), (0, 0)))


def layer_forward(state, weights, allowed, cosine, sine):
    w_query, w_key, w_value, w_out, w_gate, w_up, w_down, gains = weights
    gains = gains.astype(jnp.float32)
    rows = state.shape[0]
    group = HEADS_Q // HEADS_KV
    scale = 1.0 / math.sqrt(HEAD)
    normed = rms_scale(state, gains[0]).astype(jnp.bfloat16)
    query = product(normed, w_query)
    keys = product(normed, w_key)
    values = product(normed, w_value).astype(jnp.bfloat16).reshape(rows, HEADS_KV, HEAD)
    query_rot = (
        rotate(query.reshape(rows, HEADS_Q, HEAD), cosine, sine)
        .astype(jnp.bfloat16)
        .reshape(rows, HEADS_KV, group, HEAD)
    )
    key_rot = rotate(keys.reshape(rows, HEADS_KV, HEAD), cosine, sine).astype(jnp.bfloat16)
    scores = (
        jnp.einsum("qhgd,khd->hgqk", query_rot, key_rot, preferred_element_type=jnp.float32) * scale
    )
    scores = jnp.where(allowed[None, None], scores, NEGATIVE)
    top = jnp.max(scores, axis=-1, keepdims=True)
    unnormed = jnp.exp(scores - top)
    total = jnp.sum(unnormed, axis=-1, keepdims=True)
    probs = (unnormed / total).astype(jnp.bfloat16)
    log_total = top + jnp.log(total)
    mixed = jnp.einsum("hgqk,khd->qhgd", probs, values, preferred_element_type=jnp.float32)
    mixed = mixed.reshape(rows, HEADS_Q * HEAD).astype(jnp.bfloat16)
    resid = state + product(mixed, w_out)
    normed2 = rms_scale(resid, gains[1]).astype(jnp.bfloat16)
    gate = product(normed2, w_gate)
    lifted = product(normed2, w_up)
    hidden = (gate * jax.nn.sigmoid(gate) * lifted).astype(jnp.bfloat16)
    result = resid + product(hidden, w_down)
    return (
        result,
        (
            state,
            normed,
            query_rot,
            key_rot,
            values,
            log_total,
            mixed,
            resid,
            normed2,
            gate,
            lifted,
            hidden,
        ),
    )


def layer_backward(grad, weights, keep, allowed, cosine, sine):
    w_query, w_key, w_value, w_out, w_gate, w_up, w_down, gains = weights
    gains = gains.astype(jnp.float32)
    (
        state,
        normed,
        query_rot,
        key_rot,
        values,
        log_total,
        mixed,
        resid,
        normed2,
        gate,
        lifted,
        hidden,
    ) = keep
    rows = state.shape[0]
    group = HEADS_Q // HEADS_KV
    scale = 1.0 / math.sqrt(HEAD)
    grad_branch = grad.astype(jnp.bfloat16)
    g_down = outer_rows(hidden, grad_branch)
    grad_hidden = back_product(grad_branch, w_down)
    sigma = jax.nn.sigmoid(gate)
    grad_gate = (grad_hidden * lifted * sigma * (1.0 + gate * (1.0 - sigma))).astype(jnp.bfloat16)
    grad_lift = (grad_hidden * gate * sigma).astype(jnp.bfloat16)
    g_gate = outer_rows(normed2, grad_gate)
    g_up = outer_rows(normed2, grad_lift)
    grad_normed2 = back_product(grad_gate, w_gate) + back_product(grad_lift, w_up)
    grad_resid_norm, g_mlp = norm_back(grad_normed2, resid, gains[1])
    grad_resid = grad + grad_resid_norm
    resid_branch = grad_resid.astype(jnp.bfloat16)
    g_out = outer_rows(mixed, resid_branch)
    grad_mixed = (
        back_product(resid_branch, w_out).astype(jnp.bfloat16).reshape(rows, HEADS_KV, group, HEAD)
    )
    scores = (
        jnp.einsum("qhgd,khd->hgqk", query_rot, key_rot, preferred_element_type=jnp.float32) * scale
    )
    scores = jnp.where(allowed[None, None], scores, NEGATIVE)
    probs_full = jnp.exp(scores - log_total)
    probs = probs_full.astype(jnp.bfloat16)
    grad_probs = jnp.einsum(
        "qhgd,khd->hgqk", grad_mixed, values, preferred_element_type=jnp.float32
    )
    delta = jnp.sum(grad_probs * probs_full, axis=-1, keepdims=True)
    grad_scores = (probs_full * (grad_probs - delta)).astype(jnp.bfloat16)
    grad_qrot = (
        jnp.einsum("hgqk,khd->qhgd", grad_scores, key_rot, preferred_element_type=jnp.float32)
        * scale
    )
    grad_krot = (
        jnp.einsum("hgqk,qhgd->khd", grad_scores, query_rot, preferred_element_type=jnp.float32)
        * scale
    )
    grad_values = jnp.einsum(
        "hgqk,qhgd->khd", probs, grad_mixed, preferred_element_type=jnp.float32
    )
    grad_values = grad_values.reshape(rows, HEADS_KV * HEAD).astype(jnp.bfloat16)
    grad_query = (
        rotate_back(grad_qrot.reshape(rows, HEADS_Q, HEAD), cosine, sine)
        .reshape(rows, HEADS_Q * HEAD)
        .astype(jnp.bfloat16)
    )
    grad_keys = (
        rotate_back(grad_krot, cosine, sine).reshape(rows, HEADS_KV * HEAD).astype(jnp.bfloat16)
    )
    g_query = outer_rows(normed, grad_query)
    g_key = outer_rows(normed, grad_keys)
    g_value = outer_rows(normed, grad_values)
    grad_normed = (
        back_product(grad_query, w_query)
        + back_product(grad_keys, w_key)
        + back_product(grad_values, w_value)
    )
    grad_state_norm, g_attn = norm_back(grad_normed, state, gains[0])
    return (
        grad_resid + grad_state_norm,
        (g_query, g_key, g_value, g_out, g_gate, g_up, g_down, jnp.stack([g_attn, g_mlp])),
    )


def local(
    tokens,
    segments,
    cotangent,
    attn_gain,
    w_query,
    w_key,
    w_value,
    w_out,
    mlp_gain,
    w_gate,
    w_up,
    w_down,
):
    stacked = (w_query, w_key, w_value, w_out, w_gate, w_up, w_down)
    rows, half = w_gate.shape[1], w_gate.shape[2] // 2
    widths = [item.shape[2] for item in stacked[:4]]
    orders = exchange_orders()
    packed = [pack(*[item[level] for item in stacked]) for level in range(LAYERS)]
    gains = jnp.concatenate([attn_gain, mlp_gain], axis=0)
    gains = jnp.pad(gains, ((0, 16 - 2 * LAYERS), (0, 128 - rows)))
    first, second, all_gains = gather_all(packed[0], packed[1], gains)
    ndp, nfsdp = lax.axis_size("dp"), lax.axis_size("fsdp")
    all_gains = from_slots(all_gains.reshape(-1, 16, 128), orders[0], [0, 1], [])
    all_gains = all_gains.reshape(ndp, 16, 128, nfsdp)[:, : 2 * LAYERS, :rows, 0]
    all_gains = all_gains.transpose(1, 0, 2).reshape(2 * LAYERS, ndp * rows)
    gathered = []
    for level, slots in enumerate((first, second)):
        weights = unpack_all(slots, orders[level], rows, widths)
        gathered.append(weights + (jnp.stack([all_gains[level], all_gains[LAYERS + level]]),))
    allowed, cosine, sine = tables(segments)
    state = tokens.astype(jnp.float32)
    saved = []
    for level in range(LAYERS):
        state, keep = layer_forward(state, gathered[level], allowed, cosine, sine)
        saved.append(keep)
    output = state.astype(jnp.bfloat16)
    grad = cotangent.astype(jnp.float32) * (segments >= 0).astype(jnp.float32)[:, None]
    sums = [None] * LAYERS
    gain_sums = [None] * LAYERS
    for level in reversed(range(LAYERS)):
        grad, terms = layer_backward(grad, gathered[level], saved[level], allowed, cosine, sine)
        sums[level] = pack_all(terms[:7], orders[level], rows, widths, half)
        gain_sums[level] = terms[7]
    small = jnp.concatenate(gain_sums, axis=0).reshape(2 * LAYERS, ndp, rows)
    small = jnp.pad(small, ((0, 8 - 2 * LAYERS), (0, 0), (0, 128 - rows)))
    small = jnp.broadcast_to(small[..., None], small.shape + (nfsdp,)).transpose(1, 0, 2, 3)
    small = to_slots(small, orders[0], [8, 128], [0, 1], [])
    low, high, gain_total = scatter_all(sums[0], sums[1], small)
    shards = [unpack_shard(item, rows, widths) for item in (low, high)]
    mats = [jnp.stack([shards[level][index] for level in range(LAYERS)]) for index in range(7)]
    grad_attn = jnp.stack([gain_total[2 * level, :rows] for level in range(LAYERS)])
    grad_mlp = jnp.stack([gain_total[2 * level + 1, :rows] for level in range(LAYERS)])
    return (
        output,
        grad,
        grad_attn,
        mats[0],
        mats[1],
        mats[2],
        mats[3],
        grad_mlp,
        mats[4],
        mats[5],
        mats[6],
    )


def solution(mesh):
    placed = (
        P(("dp", "fsdp"), None),
        P(("dp", "fsdp")),
        P(("dp", "fsdp"), None),
        P(None, "dp"),
        P(None, "dp", "fsdp"),
        P(None, "dp", "fsdp"),
        P(None, "dp", "fsdp"),
        P(None, "dp", "fsdp"),
        P(None, "dp"),
        P(None, "dp", "fsdp"),
        P(None, "dp", "fsdp"),
        P(None, "dp", "fsdp"),
    )
    return jax.shard_map(
        local,
        mesh=mesh,
        in_specs=placed,
        out_specs=(
            P(("dp", "fsdp"), None),
            P(("dp", "fsdp"), None),
            P(None, "dp"),
            P(None, "dp", "fsdp"),
            P(None, "dp", "fsdp"),
            P(None, "dp", "fsdp"),
            P(None, "dp", "fsdp"),
            P(None, "dp"),
            P(None, "dp", "fsdp"),
            P(None, "dp", "fsdp"),
            P(None, "dp", "fsdp"),
        ),
        check_vma=False,
    )
```
